512 devices in a mesh: tm: 32 (over x, y), cp: 16 (over z, core).
Axes of the slice: x: 4, y: 8, z: 8, core: 2. Of those that a mesh axis runs over, the one named last changes fastest.
Arguments:
- echoes: bfloat16 [2, 128, 524288], P(None, 'cp', 'tm'), may hold values from -6 to 6
Outputs:
- channels: bfloat16 [2, 128, 64, 8192], P(None, 'cp', 'tm')
The draws below stay inside these ranges and needn't reach their ends.
All inputs are finite; a program needn't handle non-finite values.
Results may differ from the reference program's by a relative error of at most 0.0068.
Values may be sent and summed in bfloat16 or wider, within the bound.
A program may use at most 64 MiB of HBM per device.

```python
import math
import jax
import jax.numpy as jnp
from jax import lax

CHIRP = 1024
BANDS = 64
TAPS = 4096
ROWS = 128
SAMPLES = 524288


def shard_levels(rng, dims, pieces, smallest, largest):
    loudness, own = 1.0, jax.random.fold_in(rng, 6)
    for dim, blocks in pieces:
        heights = jnp.exp(jax.random.uniform(jax.random.fold_in(own, dim), (blocks,), jnp.float32, smallest / len(pieces), largest / len(pieces)))
        loudness = loudness * jnp.repeat(heights, dims[dim] // blocks).reshape([-1 if axis == dim else 1 for axis in range(len(dims))])
    return loudness


def noise(own_key, shape, scale, most, pieces=(), held_as=jnp.bfloat16):
    level = shard_levels(own_key, shape, pieces, -0.22, 0.18) if pieces else 1.0
    drawn = jax.random.normal(own_key, shape, jnp.float32) * scale * level
    return jnp.minimum(jnp.maximum(drawn, -most), most).astype(held_as)


def setup_inputs(seed: int = 0) -> dict:
    key_list = jax.random.split(jax.random.key(seed), 2)
    echoes = noise(key_list[0], (2, ROWS, SAMPLES), 1.0, 6.0, ((1, 16), (2, 32)))
    return dict(echoes=echoes)


def chirp_tables(width):
    source = jnp.arange(2 * width, dtype=jnp.int32)[:, None]
    target = jnp.arange(width, dtype=jnp.int32)[None, :]
    lag_index = target + width - source
    inside = (lag_index >= 0) & (lag_index < width)
    offset = lag_index - width // 2
    residue = offset * offset % (2 * width)
    phase = jnp.pi * residue.astype(jnp.float32) / width
    factor = 1.0 / math.sqrt(width)
    real_table = jnp.where(inside, jnp.cos(phase) * factor, 0.0).astype(jnp.bfloat16)
    imag_table = jnp.where(inside, jnp.sin(phase) * factor, 0.0).astype(jnp.bfloat16)
    return (real_table, imag_table)

def prototype(taps, bands):
    sample = jnp.arange(taps, dtype=jnp.int32).astype(jnp.float32)
    centred = (sample - (taps - 1) / 2.0) / bands
    window = 0.5 - 0.5 * jnp.cos(2.0 * jnp.pi * (sample + 0.5) / taps)
    return (jnp.sinc(centred) * window / math.sqrt(bands)).astype(jnp.bfloat16)

def dft_tables(bands):
    column = jnp.arange(bands, dtype=jnp.int32)
    residue = column[:, None] * column[None, :] % bands
    angle = 2.0 * jnp.pi * residue.astype(jnp.float32) / bands
    return (jnp.cos(angle).astype(jnp.bfloat16), jnp.sin(angle).astype(jnp.bfloat16))

def compress(extended, real_table, imag_table, width):
    rows = extended.shape[1]
    blocks = extended.shape[2] // width - 1
    framed = extended.reshape(2, rows, blocks + 1, width)
    paired = jnp.concatenate([framed[:, :, :-1], framed[:, :, 1:]], axis=3).reshape(2, rows * blocks, 2 * width)
    paired = paired.astype(jnp.float32)
    real_wide = real_table.astype(jnp.float32)
    imag_wide = imag_table.astype(jnp.float32)
    real_part = jnp.dot(paired[0], real_wide, preferred_element_type=jnp.float32) - jnp.dot(paired[1], imag_wide, preferred_element_type=jnp.float32)
    imag_part = jnp.dot(paired[0], imag_wide, preferred_element_type=jnp.float32) + jnp.dot(paired[1], real_wide, preferred_element_type=jnp.float32)
    return jnp.stack([real_part, imag_part]).reshape(2, rows, blocks * width).astype(jnp.bfloat16)

def channelize(extended, taps, bands):
    rows = extended.shape[1]
    depth = taps // bands
    count = extended.shape[2] // bands - depth + 1
    frames = extended.reshape(2, rows, count + depth - 1, bands).transpose(0, 1, 3, 2).astype(jnp.float32)
    weights = prototype(taps, bands).astype(jnp.float32).reshape(depth, bands)

    def add_tap(tap_index, running):
        piece = lax.dynamic_slice_in_dim(frames, tap_index, count, 3)
        column = lax.dynamic_slice_in_dim(weights, tap_index, 1, 0).reshape(bands, 1)
        return running + piece * column
    folded = lax.fori_loop(0, depth, add_tap, jnp.zeros((2, rows, bands, count), jnp.float32)).astype(jnp.bfloat16)
    cosine, sine = dft_tables(bands)
    cosine = cosine.astype(jnp.float32)
    sine = sine.astype(jnp.float32)
    folded = folded.astype(jnp.float32)

    def mix(table, part):
        return jnp.einsum('mb,rbf->rmf', table, part)
    real_part = mix(cosine, folded[0]) + mix(sine, folded[1])
    imag_part = mix(cosine, folded[1]) - mix(sine, folded[0])
    return jnp.stack([real_part, imag_part]).astype(jnp.bfloat16)

def reference(echoes):
    real_table, imag_table = chirp_tables(CHIRP)

    def one_row(row_pair):
        extended = jnp.concatenate([jnp.zeros((2, CHIRP), jnp.bfloat16), row_pair], axis=1)[:, None, :]
        compressed = compress(extended, real_table, imag_table, CHIRP)
        padded = jnp.concatenate([jnp.zeros((2, 1, TAPS - BANDS), jnp.bfloat16), compressed], axis=2)
        return channelize(padded, TAPS, BANDS)[:, 0]
    outputs = lax.map(one_row, jnp.transpose(echoes, (1, 0, 2)))
    return jnp.transpose(outputs, (1, 0, 2, 3))
```

```python
import math

import jax
import jax.numpy as jnp
import ml_dtypes
import numpy as np
from jax import lax
from jax.experimental import pallas as pl
from jax.experimental.pallas import tpu as pltpu
from jax.sharding import PartitionSpec as P

CHIRP = 1024
BANDS = 64
TAPS = 4096
MESH = pl.DeviceIdType.MESH

FRAME = 128
SPAN = 41
HALO = SPAN - 1
WEIGHT_PARTS = 4


def rounded(values):
    return np.asarray(values, np.float64).astype(ml_dtypes.bfloat16).astype(np.float64)


def weights():
    lag = np.arange(CHIRP)
    phase = math.pi * ((lag - CHIRP // 2) ** 2 % (2 * CHIRP)) / CHIRP
    scale = 1.0 / math.sqrt(CHIRP)
    chirp = rounded(np.cos(phase) * scale) + 1j * rounded(np.sin(phase) * scale)
    tap = np.arange(TAPS)
    window = 0.5 - 0.5 * np.cos(2.0 * np.pi * (tap + 0.5) / TAPS)
    prototype = rounded(np.sinc((tap - (TAPS - 1) / 2.0) / BANDS) * window / math.sqrt(BANDS))
    column = np.arange(BANDS)
    angle = 2.0 * np.pi * (column[:, None] * column[None, :] % BANDS) / BANDS
    table = rounded(np.cos(angle)) - 1j * rounded(np.sin(angle))
    modulated = prototype[None, :] * np.tile(table, (1, TAPS // BANDS))
    length = 2 * TAPS
    filters = np.fft.ifft(
        np.fft.fft(modulated, length, axis=1) * np.fft.fft(chirp[::-1], length)[None, :], axis=1
    )[:, : TAPS + CHIRP - 1]
    samples = SPAN * FRAME
    placed = np.zeros((2, samples, BANDS), np.complex128)
    for parity in range(2):
        first = (SPAN - 1) * FRAME + (parity + 1) * BANDS - (TAPS + CHIRP - 1)
        placed[parity, first : first + TAPS + CHIRP - 1] = filters.T
    real, imag = placed.real, placed.imag
    parts = np.stack(
        [np.stack([real, imag], axis=2), np.stack([-imag, real], axis=2)]
    )
    parts = parts.reshape(2, 2, SPAN, FRAME, 2, BANDS // 2, 2)
    parts = parts.transpose(2, 0, 3, 1, 6, 4, 5)
    return parts.reshape(SPAN, 2 * FRAME, 4 * BANDS).astype(np.float32).astype(ml_dtypes.bfloat16)


def kernel(
    count, x_ref, w_ref, o_ref, own, halo, weight, pairs, total, times, turned, outgoing,
    own_sem, weight_sem, halo_send, halo_recv, send_sem, recv_sem, local_sem,
):
    me = lax.axis_index("tm")
    frames = own.shape[1] // FRAME
    half = frames // 2
    quarter = half // 2
    steps = 2 * frames

    load = pltpu.make_async_copy(x_ref, own, own_sem)
    load.start()
    loads = []
    bounds = [SPAN * i // WEIGHT_PARTS for i in range(WEIGHT_PARTS + 1)]
    for i in range(WEIGHT_PARTS):
        piece = pl.ds(bounds[i], bounds[i + 1] - bounds[i])
        loads.append(
            pltpu.make_async_copy(w_ref.at[piece], weight.at[piece], weight_sem.at[i])
        )
        loads[-1].start()

    barrier = pltpu.get_barrier_semaphore()
    for shift in range(1, count):
        pl.semaphore_signal(
            barrier, inc=1, device_id={"tm": lax.rem(me + shift, count)}, device_id_type=MESH
        )
    pl.semaphore_wait(barrier, count - 1)

    edge = pltpu.make_async_remote_copy(
        src_ref=x_ref.at[:, pl.ds((frames - HALO) * FRAME, HALO * FRAME)],
        dst_ref=halo,
        send_sem=halo_send,
        recv_sem=halo_recv,
        device_id={"tm": lax.rem(me + 1, count)},
        device_id_type=MESH,
    )

    @pl.when(me < count - 1)
    def _():
        edge.start()

    def pair(earlier, later):
        earlier, later = earlier.astype(jnp.float32), later.astype(jnp.float32)
        return jnp.concatenate(
            [
                jnp.concatenate([earlier[:8], later[:8]], axis=0),
                jnp.concatenate([earlier[8:], later[8:]], axis=0),
            ],
            axis=1,
        ).astype(jnp.bfloat16)

    def frame_of(ref, index):
        return ref[:, pl.ds(pl.multiple_of(index * FRAME, FRAME), FRAME)]

    def pair_own(first, last):
        def one(index, carry):
            pairs[HALO + index] = pair(frame_of(own, index), frame_of(own, index + quarter))
            return carry

        lax.fori_loop(first, last, one, 0, unroll=8)

    def pair_halo():
        def both(index, carry):
            pairs[index] = pair(frame_of(halo, index), frame_of(halo, index + quarter))
            return carry

        def mixed(index, carry):
            pairs[index] = pair(frame_of(halo, index), frame_of(own, index + quarter - HALO))
            return carry

        lax.fori_loop(0, HALO - quarter, both, 0, unroll=8)
        lax.fori_loop(HALO - quarter, HALO, mixed, 0, unroll=8)

    load.wait()
    pair_own(half - HALO, half + quarter)

    def one_half(turn, carry):
        side = 1 - turn
        @pl.when(turn == 1)
        def _():
            pair_own(0, half - HALO)

            @pl.when(me > 0)
            def _():
                edge.wait_recv()

            @pl.when(me == 0)
            def _():
                halo[...] = jnp.zeros_like(halo)

            pair_halo()

        for i in range(WEIGHT_PARTS):
            @pl.when(turn == 0)
            def _():
                loads[i].wait()

            lag = bounds[i]
            amount = bounds[i + 1] - bounds[i]
            first = side * half
            left = jnp.concatenate(
                [
                    pairs[pl.ds(first + lag + j, quarter)].reshape(quarter * 16, 2 * FRAME)
                    for j in range(amount)
                ],
                axis=1,
            )
            right = weight[pl.ds(lag, amount)].reshape(amount * 2 * FRAME, 4 * BANDS)
            product = jnp.dot(left, right, preferred_element_type=jnp.float32)
            if i == 0:
                total[...] = product
            else:
                total[...] += product

        for v in range(quarter):
            for late in range(2):
                for parity in range(2):
                    row = ((late * quarter + v) * 2 + parity) * 8
                    times[row : row + 8, :] = total[
                        v * 16 + late * 8 : v * 16 + late * 8 + 8, parity * 128 : parity * 128 + 128
                    ]
        for r in range(8):
            across = times[pl.ds(r, frames, stride=8), :].T
            for band in range(2):
                turned[pl.ds(2 * r + band, 2 * count, stride=16), :] = across[
                    band * 64 : band * 64 + 64
                ]
        outgoing[side] = turned[...].astype(jnp.bfloat16).reshape(2, count, 16, frames)

        start = pl.multiple_of(me * steps + side * frames, frames)
        for shift in range(1, count):
            to = lax.rem(me + shift, count)
            pltpu.make_async_remote_copy(
                src_ref=outgoing.at[side, :, to],
                dst_ref=o_ref.at[:, :, pl.ds(start, frames)],
                send_sem=send_sem.at[side, shift],
                recv_sem=recv_sem.at[side, shift],
                device_id={"tm": to},
                device_id_type=MESH,
            ).start()
        pltpu.make_async_copy(
            outgoing.at[side, :, me], o_ref.at[:, :, pl.ds(start, frames)], local_sem.at[side]
        ).start()
        return carry

    lax.fori_loop(0, 2, one_half, 0)

    @pl.when(me < count - 1)
    def _():
        edge.wait_send()

    for turn in range(2):
        side = 1 - turn
        start = pl.multiple_of(me * steps + side * frames, frames)
        for shift in range(1, count):
            to = lax.rem(me + shift, count)
            pltpu.make_async_remote_copy(
                src_ref=outgoing.at[side, :, to],
                dst_ref=o_ref.at[:, :, pl.ds(start, frames)],
                send_sem=send_sem.at[side, shift],
                recv_sem=recv_sem.at[side, shift],
                device_id={"tm": to},
                device_id_type=MESH,
            ).wait()
        pltpu.make_async_copy(
            outgoing.at[side, :, me], o_ref.at[:, :, pl.ds(start, frames)], local_sem.at[side]
        ).wait()


def solution(mesh):
    count = mesh.shape["tm"]
    table = weights()

    def shards(echoes):
        parts, rows, samples = echoes.shape
        frames = samples // FRAME
        quarter = frames // 4
        result = pl.pallas_call(
            lambda *refs: kernel(count, *refs),
            out_shape=jax.ShapeDtypeStruct((2, 16, count * 2 * frames), jnp.bfloat16),
            in_specs=[pl.BlockSpec(memory_space=pl.ANY)] * 2,
            out_specs=pl.BlockSpec(memory_space=pl.ANY),
            scratch_shapes=[
                pltpu.VMEM((16, samples), jnp.bfloat16),
                pltpu.VMEM((16, HALO * FRAME), jnp.bfloat16),
                pltpu.VMEM(table.shape, jnp.bfloat16),
                pltpu.VMEM((HALO + frames - quarter, 16, 2 * FRAME), jnp.bfloat16),
                pltpu.VMEM((quarter * 16, 4 * BANDS), jnp.float32),
                pltpu.VMEM((frames * 8, 2 * BANDS), jnp.float32),
                pltpu.VMEM((2 * count * 16, frames), jnp.float32),
                pltpu.VMEM((2, 2, count, 16, frames), jnp.bfloat16),
                pltpu.SemaphoreType.DMA,
                pltpu.SemaphoreType.DMA((WEIGHT_PARTS,)),
                pltpu.SemaphoreType.DMA,
                pltpu.SemaphoreType.DMA,
                pltpu.SemaphoreType.DMA((2, count)),
                pltpu.SemaphoreType.DMA((2, count)),
                pltpu.SemaphoreType.DMA((2,)),
            ],
            compiler_params=pltpu.CompilerParams(
                collective_id=0, has_side_effects=True, vmem_limit_bytes=60 << 20
            ),
            name="radar",
        )(echoes.reshape(parts * rows, samples), jnp.asarray(table))
        return result.reshape(2, rows, 2, count * 2 * frames)

    return jax.shard_map(
        shards,
        mesh=mesh,
        in_specs=(P(None, "cp", "tm"),),
        out_specs=P(None, "cp", "tm", None),
        check_vma=False,
    )
```

```python
import math

import jax
import jax.numpy as jnp
import ml_dtypes
import numpy as np
from jax import lax
from jax.experimental import pallas as pl
from jax.experimental.pallas import tpu as pltpu
from jax.sharding import PartitionSpec as P

CHIRP = 1024
BANDS = 64
TAPS = 4096
MESH = pl.DeviceIdType.MESH

FRAME = 128
SPAN = 41
HALO = SPAN - 1
GROUP = 10
GROUPS = (SPAN - 1) // GROUP


def rounded(values):
    return np.asarray(values, np.float64).astype(ml_dtypes.bfloat16).astype(np.float64)


def weights():
    lag = np.arange(CHIRP)
    phase = math.pi * ((lag - CHIRP // 2) ** 2 % (2 * CHIRP)) / CHIRP
    scale = 1.0 / math.sqrt(CHIRP)
    chirp = rounded(np.cos(phase) * scale) + 1j * rounded(np.sin(phase) * scale)
    tap = np.arange(TAPS)
    window = 0.5 - 0.5 * np.cos(2.0 * np.pi * (tap + 0.5) / TAPS)
    prototype = rounded(np.sinc((tap - (TAPS - 1) / 2.0) / BANDS) * window / math.sqrt(BANDS))
    column = np.arange(BANDS)
    angle = 2.0 * np.pi * (column[:, None] * column[None, :] % BANDS) / BANDS
    table = rounded(np.cos(angle)) - 1j * rounded(np.sin(angle))
    modulated = prototype[None, :] * np.tile(table, (1, TAPS // BANDS))
    length = 2 * TAPS
    filters = np.fft.ifft(
        np.fft.fft(modulated, length, axis=1) * np.fft.fft(chirp[::-1], length)[None, :], axis=1
    )[:, : TAPS + CHIRP - 1]
    samples = SPAN * FRAME
    placed = np.zeros((2, samples, BANDS), np.complex128)
    for parity in range(2):
        first = (SPAN - 1) * FRAME + (parity + 1) * BANDS - (TAPS + CHIRP - 1)
        placed[parity, first : first + TAPS + CHIRP - 1] = filters.T
    real, imag = placed.real, placed.imag
    parts = np.stack(
        [np.stack([real, imag], axis=2), np.stack([-imag, real], axis=2)]
    )
    parts = parts.reshape(2, 2, SPAN, FRAME, 2, BANDS // 2, 2)
    parts = parts.transpose(2, 0, 3, 1, 6, 4, 5)
    return parts.reshape(SPAN, 2 * FRAME, 4 * BANDS).astype(np.float32).astype(ml_dtypes.bfloat16)


def kernel(
    count, x_ref, w_ref, o_ref, own, halo, weight, pairs, total, times, turned, outgoing,
    own_sem, weight_sem, halo_send, halo_recv, send_sem, recv_sem, local_sem,
):
    me = lax.axis_index("tm")
    frames = own.shape[1] // FRAME
    half = frames // 2
    quarter = half // 2
    steps = 2 * frames

    load = pltpu.make_async_copy(x_ref, own, own_sem)
    load.start()

    def weight_load(group):
        piece = pl.ds(0, 1) if group is None else pl.ds(1 + group * GROUP, GROUP)
        sem = weight_sem.at[GROUPS if group is None else group]
        return pltpu.make_async_copy(w_ref.at[piece], weight.at[piece], sem)

    weight_load(None).start()
    for group in range(GROUPS):
        weight_load(group).start()

    barrier = pltpu.get_barrier_semaphore()
    for shift in range(1, count):
        pl.semaphore_signal(
            barrier, inc=1, device_id={"tm": lax.rem(me + shift, count)}, device_id_type=MESH
        )

    edge = pltpu.make_async_remote_copy(
        src_ref=x_ref.at[:, pl.ds((frames - HALO) * FRAME, HALO * FRAME)],
        dst_ref=halo,
        send_sem=halo_send,
        recv_sem=halo_recv,
        device_id={"tm": lax.rem(me + 1, count)},
        device_id_type=MESH,
    )

    def greet():
        pl.semaphore_wait(barrier, count - 1)

        @pl.when(me < count - 1)
        def _():
            edge.start()

    def pair(earlier, later):
        earlier, later = earlier.astype(jnp.float32), later.astype(jnp.float32)
        return jnp.concatenate(
            [
                jnp.concatenate([earlier[:8], later[:8]], axis=0),
                jnp.concatenate([earlier[8:], later[8:]], axis=0),
            ],
            axis=1,
        ).astype(jnp.bfloat16)

    def frame_of(ref, index):
        return ref[:, pl.ds(pl.multiple_of(index * FRAME, FRAME), FRAME)]

    def pair_own(first, last):
        def one(index, carry):
            pairs[HALO + index] = pair(frame_of(own, index), frame_of(own, index + quarter))
            return carry

        lax.fori_loop(first, last, one, 0, unroll=8)

    def pair_halo():
        def both(index, carry):
            pairs[index] = pair(frame_of(halo, index), frame_of(halo, index + quarter))
            return carry

        def mixed(index, carry):
            pairs[index] = pair(frame_of(halo, index), frame_of(own, index + quarter - HALO))
            return carry

        lax.fori_loop(0, HALO - quarter, both, 0, unroll=8)
        lax.fori_loop(HALO - quarter, HALO, mixed, 0, unroll=8)

    load.wait()
    pair_own(half - HALO, half + quarter)

    def one_half(turn, carry):
        side = 1 - turn
        @pl.when(turn == 1)
        def _():
            pair_own(0, half - HALO)

            @pl.when(me > 0)
            def _():
                edge.wait_recv()

            @pl.when(me == 0)
            def _():
                halo[...] = jnp.zeros_like(halo)

            pair_halo()

        first = side * half

        def product(lag, amount):
            left = jnp.concatenate(
                [
                    pairs[pl.ds(first + lag + j, quarter)].reshape(quarter * 16, 2 * FRAME)
                    for j in range(amount)
                ],
                axis=1,
            )
            right = weight[pl.ds(lag, amount)].reshape(amount * 2 * FRAME, 4 * BANDS)
            return jnp.dot(left, right, preferred_element_type=jnp.float32)

        @pl.when(turn == 0)
        def _():
            weight_load(None).wait()

        total[...] = product(0, 1)

        def one_group(group, carry):
            @pl.when(turn == 0)
            def _():
                weight_load(group).wait()

            total[...] += product(1 + group * GROUP, GROUP)

            @pl.when((turn == 0) & (group == 0))
            def _():
                greet()

            return carry

        lax.fori_loop(0, GROUPS, one_group, 0)

        for v in range(quarter):
            for late in range(2):
                for parity in range(2):
                    row = ((late * quarter + v) * 2 + parity) * 8
                    times[row : row + 8, :] = total[
                        v * 16 + late * 8 : v * 16 + late * 8 + 8, parity * 128 : parity * 128 + 128
                    ]
        for r in range(8):
            across = times[pl.ds(r, frames, stride=8), :].T
            for band in range(2):
                turned[pl.ds(2 * r + band, 2 * count, stride=16), :] = across[
                    band * 64 : band * 64 + 64
                ]
        outgoing[side] = turned[...].astype(jnp.bfloat16).reshape(2, count, 8, 2, frames)

        start = pl.multiple_of(me * steps + side * frames, frames)
        for shift in range(1, count):
            to = lax.rem(me + shift, count)
            pltpu.make_async_remote_copy(
                src_ref=outgoing.at[side, :, to],
                dst_ref=o_ref.at[:, :, :, pl.ds(start, frames)],
                send_sem=send_sem.at[side, shift],
                recv_sem=recv_sem.at[side, shift],
                device_id={"tm": to},
                device_id_type=MESH,
            ).start()
        pltpu.make_async_copy(
            outgoing.at[side, :, me], o_ref.at[:, :, :, pl.ds(start, frames)], local_sem.at[side]
        ).start()
        return carry

    lax.fori_loop(0, 2, one_half, 0)

    @pl.when(me < count - 1)
    def _():
        edge.wait_send()

    for turn in range(2):
        side = 1 - turn
        start = pl.multiple_of(me * steps + side * frames, frames)
        for shift in range(1, count):
            to = lax.rem(me + shift, count)
            pltpu.make_async_remote_copy(
                src_ref=outgoing.at[side, :, to],
                dst_ref=o_ref.at[:, :, :, pl.ds(start, frames)],
                send_sem=send_sem.at[side, shift],
                recv_sem=recv_sem.at[side, shift],
                device_id={"tm": to},
                device_id_type=MESH,
            ).wait()
        pltpu.make_async_copy(
            outgoing.at[side, :, me], o_ref.at[:, :, :, pl.ds(start, frames)], local_sem.at[side]
        ).wait()


def solution(mesh):
    count = mesh.shape["tm"]
    table = weights()

    def shards(echoes):
        parts, rows, samples = echoes.shape
        frames = samples // FRAME
        quarter = frames // 4
        result = pl.pallas_call(
            lambda *refs: kernel(count, *refs),
            out_shape=pltpu.VMEM((2, rows, 2, count * 2 * frames), jnp.bfloat16),
            in_specs=[pl.BlockSpec(memory_space=pl.ANY)] * 2,
            out_specs=pl.BlockSpec(memory_space=pltpu.VMEM),
            scratch_shapes=[
                pltpu.VMEM((16, samples), jnp.bfloat16),
                pltpu.VMEM((16, HALO * FRAME), jnp.bfloat16),
                pltpu.VMEM(table.shape, jnp.bfloat16),
                pltpu.VMEM((HALO + frames - quarter, 16, 2 * FRAME), jnp.bfloat16),
                pltpu.VMEM((quarter * 16, 4 * BANDS), jnp.float32),
                pltpu.VMEM((frames * 8, 2 * BANDS), jnp.float32),
                pltpu.VMEM((2 * count * 16, frames), jnp.float32),
                pltpu.VMEM((2, 2, count, 8, 2, frames), jnp.bfloat16),
                pltpu.SemaphoreType.DMA,
                pltpu.SemaphoreType.DMA((GROUPS + 1,)),
                pltpu.SemaphoreType.DMA,
                pltpu.SemaphoreType.DMA,
                pltpu.SemaphoreType.DMA((2, count)),
                pltpu.SemaphoreType.DMA((2, count)),
                pltpu.SemaphoreType.DMA((2,)),
            ],
            compiler_params=pltpu.CompilerParams(
                collective_id=0, has_side_effects=True, vmem_limit_bytes=60 << 20
            ),
            name="radar",
        )(echoes.reshape(parts * rows, samples), jnp.asarray(table))
        return result

    return jax.shard_map(
        shards,
        mesh=mesh,
        in_specs=(P(None, "cp", "tm"),),
        out_specs=P(None, "cp", "tm", None),
        check_vma=False,
    )
```

```python
import math

import jax
import jax.numpy as jnp
import ml_dtypes
import numpy as np
from jax import lax
from jax.experimental import pallas as pl
from jax.experimental.pallas import tpu as pltpu
from jax.sharding import PartitionSpec as P

CHIRP = 1024
BANDS = 64
TAPS = 4096
MESH = pl.DeviceIdType.MESH

FRAME = 128
SPAN = 41
HALO = SPAN - 1
GROUP = 20
GROUPS = (SPAN - 1) // GROUP
APART = 16


def rounded(values):
    return np.asarray(values, np.float64).astype(ml_dtypes.bfloat16).astype(np.float64)


def weights():
    lag = np.arange(CHIRP)
    phase = math.pi * ((lag - CHIRP // 2) ** 2 % (2 * CHIRP)) / CHIRP
    scale = 1.0 / math.sqrt(CHIRP)
    chirp = rounded(np.cos(phase) * scale) + 1j * rounded(np.sin(phase) * scale)
    tap = np.arange(TAPS)
    window = 0.5 - 0.5 * np.cos(2.0 * np.pi * (tap + 0.5) / TAPS)
    prototype = rounded(np.sinc((tap - (TAPS - 1) / 2.0) / BANDS) * window / math.sqrt(BANDS))
    column = np.arange(BANDS)
    angle = 2.0 * np.pi * (column[:, None] * column[None, :] % BANDS) / BANDS
    table = rounded(np.cos(angle)) - 1j * rounded(np.sin(angle))
    modulated = prototype[None, :] * np.tile(table, (1, TAPS // BANDS))
    length = 2 * TAPS
    filters = np.fft.ifft(
        np.fft.fft(modulated, length, axis=1) * np.fft.fft(chirp[::-1], length)[None, :], axis=1
    )[:, : TAPS + CHIRP - 1]
    samples = SPAN * FRAME
    placed = np.zeros((2, samples, BANDS), np.complex128)
    for parity in range(2):
        first = (SPAN - 1) * FRAME + (parity + 1) * BANDS - (TAPS + CHIRP - 1)
        placed[parity, first : first + TAPS + CHIRP - 1] = filters.T
    real, imag = placed.real, placed.imag
    parts = np.stack(
        [np.stack([real, imag], axis=2), np.stack([-imag, real], axis=2)]
    )
    parts = parts.reshape(2, 2, SPAN, FRAME, 2, BANDS // 2, 2)
    parts = parts.transpose(2, 0, 3, 1, 6, 4, 5)
    return parts.reshape(SPAN, 2 * FRAME, 4 * BANDS).astype(np.float32).astype(ml_dtypes.bfloat16)


def kernel(
    count, x_ref, w_ref, o_ref, own, weight, tiles, total, times, turned, outgoing,
    own_sem, weight_sem, halo_send, halo_recv, send_sem, recv_sem, local_sem,
):
    me = lax.axis_index("tm")
    frames = own.shape[1] // FRAME - HALO
    half = frames // 2
    block = APART * 16

    load = pltpu.make_async_copy(
        x_ref, own.at[:, pl.ds(HALO * FRAME, frames * FRAME)], own_sem
    )
    load.start()

    def weight_load(group):
        piece = pl.ds(0, 1) if group is None else pl.ds(1 + group * GROUP, GROUP)
        sem = weight_sem.at[GROUPS if group is None else group]
        return pltpu.make_async_copy(w_ref.at[piece], weight.at[piece], sem)

    for group in reversed(range(GROUPS)):
        weight_load(group).start()
    weight_load(None).start()

    barrier = pltpu.get_barrier_semaphore()
    for shift in range(1, count):
        pl.semaphore_signal(
            barrier, inc=1, device_id={"tm": lax.rem(me + shift, count)}, device_id_type=MESH
        )

    def edge(group):
        first = 1 + group * GROUP if group else 0
        size = (HALO if group == GROUPS - 1 else 1 + (group + 1) * GROUP) - first
        return pltpu.make_async_remote_copy(
            src_ref=x_ref.at[:, pl.ds((frames - HALO + first) * FRAME, size * FRAME)],
            dst_ref=own.at[:, pl.ds(first * FRAME, size * FRAME)],
            send_sem=halo_send.at[group],
            recv_sem=halo_recv.at[group],
            device_id={"tm": lax.rem(me + 1, count)},
            device_id_type=MESH,
        )

    def greet():
        pl.semaphore_wait(barrier, count - 1)

        @pl.when(me < count - 1)
        def _():
            for group in reversed(range(GROUPS)):
                edge(group).start()

    def arrange(first, last):
        def one(index, carry):
            four = [
                own[:, pl.ds(pl.multiple_of((index + j * APART) * FRAME, FRAME), FRAME)].astype(
                    jnp.float32
                )
                for j in range(4)
            ]
            for rows in range(2):
                tiles[rows, index] = jnp.concatenate(
                    [
                        jnp.concatenate(
                            [f[part * 8 + rows * 4 : part * 8 + rows * 4 + 4] for f in four], axis=0
                        )
                        for part in range(2)
                    ],
                    axis=1,
                ).astype(jnp.bfloat16)
            return carry

        lax.fori_loop(first, last, one, 0, unroll=7)

    def product(side, rows, lag, amount):
        left = jnp.concatenate(
            [
                tiles[rows, pl.ds(side * half + lag + j, APART)].reshape(block, 2 * FRAME)
                for j in range(amount)
            ],
            axis=1,
        )
        right = weight[pl.ds(lag, amount)].reshape(amount * 2 * FRAME, 4 * BANDS)
        return jnp.dot(left, right, preferred_element_type=jnp.float32)

    def send(side, rows, chunk, shift):
        to = lax.rem(me + shift, count)
        start = pl.multiple_of((me * 2 + side) * frames, frames)
        return pltpu.make_async_remote_copy(
            src_ref=outgoing.at[chunk, :, to],
            dst_ref=o_ref.at[:, pl.ds(rows * 4, 4), :, pl.ds(start, frames)],
            send_sem=send_sem.at[chunk],
            recv_sem=recv_sem.at[chunk],
            device_id={"tm": to},
            device_id_type=MESH,
        )

    def keep(side, rows, chunk):
        start = pl.multiple_of((me * 2 + side) * frames, frames)
        return pltpu.make_async_copy(
            outgoing.at[chunk, :, me],
            o_ref.at[:, pl.ds(rows * 4, 4), :, pl.ds(start, frames)],
            local_sem.at[chunk],
        )

    load.wait()
    arrange(half, HALO + frames - 3 * APART)
    greet()

    def one_chunk(chunk, carry):
        side, rows = 1 - chunk // 2, chunk % 2
        total[...] = jnp.zeros_like(total)

        def one_group(step, carry):
            group = GROUPS - 1 - step

            @pl.when(chunk == 0)
            def _():
                weight_load(group).wait()

            for part in range(GROUPS):
                @pl.when((chunk == 2) & (group == part))
                def _():
                    @pl.when(me > 0)
                    def _():
                        edge(part).wait_recv()

                    if part == GROUPS - 1:
                        @pl.when(me == 0)
                        def _():
                            own[:, : HALO * FRAME] = jnp.zeros((16, HALO * FRAME), own.dtype)

                    arrange(
                        1 + part * GROUP if part else 0,
                        HALO + APART if part == GROUPS - 1 else 1 + (part + 1) * GROUP,
                    )

            total[...] += product(side, rows, 1 + group * GROUP, GROUP)
            return carry

        lax.fori_loop(0, GROUPS, one_group, 0)

        @pl.when(chunk == 0)
        def _():
            weight_load(None).wait()

        total[...] += product(side, rows, 0, 1)

        for v in range(APART):
            for upper in range(2):
                for parity in range(2):
                    row = (upper * 2 * APART + v * 2 + parity) * 8
                    times[row : row + 8, :] = total[
                        v * 16 + upper * 8 : v * 16 + upper * 8 + 8,
                        parity * 128 : parity * 128 + 128,
                    ]
        for r in range(4):
            across = jnp.concatenate(
                [
                    times[pl.ds(j // 2 * 16 * APART + j % 2 * 4 + r, 2 * APART, stride=8), :]
                    for j in range(4)
                ],
                axis=0,
            ).T
            for band in range(2):
                turned[pl.ds(2 * r + band, 2 * count, stride=8), :] = across[
                    band * 64 : band * 64 + 64
                ]
        outgoing[chunk] = turned[...].astype(jnp.bfloat16).reshape(2, count, 4, 2, frames)
        for shift in range(1, count):
            send(side, rows, chunk, shift).start()
        keep(side, rows, chunk).start()
        return carry

    lax.fori_loop(0, 4, one_chunk, 0)

    @pl.when(me < count - 1)
    def _():
        for group in range(GROUPS):
            edge(group).wait_send()

    def finish(chunk, carry):
        side, rows = 1 - chunk // 2, chunk % 2
        others = outgoing.at[chunk, :, pl.ds(0, count - 1)]
        pltpu.make_async_copy(others, others, recv_sem.at[chunk]).wait()
        pltpu.make_async_copy(others, others, send_sem.at[chunk]).wait()
        keep(side, rows, chunk).wait()
        return carry

    lax.fori_loop(0, 4, finish, 0)


def solution(mesh):
    count = mesh.shape["tm"]
    table = weights()

    def shards(echoes):
        parts, rows, samples = echoes.shape
        frames = samples // FRAME
        result = pl.pallas_call(
            lambda *refs: kernel(count, *refs),
            out_shape=pltpu.VMEM((2, rows, 2, count * 2 * frames), jnp.bfloat16),
            in_specs=[pl.BlockSpec(memory_space=pl.ANY)] * 2,
            out_specs=pl.BlockSpec(memory_space=pltpu.VMEM),
            scratch_shapes=[
                pltpu.VMEM((16, HALO * FRAME + samples), jnp.bfloat16),
                pltpu.VMEM(table.shape, jnp.bfloat16),
                pltpu.VMEM((2, HALO + frames - 3 * APART, 16, 2 * FRAME), jnp.bfloat16),
                pltpu.VMEM((APART * 16, 4 * BANDS), jnp.float32),
                pltpu.VMEM((frames * 4, 2 * BANDS), jnp.float32),
                pltpu.VMEM((2 * count * 8, frames), jnp.float32),
                pltpu.VMEM((4, 2, count, 4, 2, frames), jnp.bfloat16),
                pltpu.SemaphoreType.DMA,
                pltpu.SemaphoreType.DMA((GROUPS + 1,)),
                pltpu.SemaphoreType.DMA((GROUPS,)),
                pltpu.SemaphoreType.DMA((GROUPS,)),
                pltpu.SemaphoreType.DMA((4,)),
                pltpu.SemaphoreType.DMA((4,)),
                pltpu.SemaphoreType.DMA((4,)),
            ],
            compiler_params=pltpu.CompilerParams(
                collective_id=0, has_side_effects=True, vmem_limit_bytes=60 << 20
            ),
            name="radar",
        )(echoes.reshape(parts * rows, samples), jnp.asarray(table))
        return result

    return jax.shard_map(
        shards,
        mesh=mesh,
        in_specs=(P(None, "cp", "tm"),),
        out_specs=P(None, "cp", "tm", None),
        check_vma=False,
    )
```

```python
import math

import jax
import jax.numpy as jnp
import ml_dtypes
import numpy as np
from jax import lax
from jax.experimental import pallas as pl
from jax.experimental.pallas import tpu as pltpu
from jax.sharding import PartitionSpec as P

CHIRP = 1024
BANDS = 64
TAPS = 4096
MESH = pl.DeviceIdType.MESH

FRAME = 128
SPAN = 41
HALO = SPAN - 1
GROUP = 20
GROUPS = (SPAN - 1) // GROUP
APART = 16


def rounded(values):
    return np.asarray(values, np.float64).astype(ml_dtypes.bfloat16).astype(np.float64)


def weights():
    lag = np.arange(CHIRP)
    phase = math.pi * ((lag - CHIRP // 2) ** 2 % (2 * CHIRP)) / CHIRP
    scale = 1.0 / math.sqrt(CHIRP)
    chirp = rounded(np.cos(phase) * scale) + 1j * rounded(np.sin(phase) * scale)
    tap = np.arange(TAPS)
    window = 0.5 - 0.5 * np.cos(2.0 * np.pi * (tap + 0.5) / TAPS)
    prototype = rounded(np.sinc((tap - (TAPS - 1) / 2.0) / BANDS) * window / math.sqrt(BANDS))
    column = np.arange(BANDS)
    angle = 2.0 * np.pi * (column[:, None] * column[None, :] % BANDS) / BANDS
    table = rounded(np.cos(angle)) - 1j * rounded(np.sin(angle))
    modulated = prototype[None, :] * np.tile(table, (1, TAPS // BANDS))
    length = 2 * TAPS
    filters = np.fft.ifft(
        np.fft.fft(modulated, length, axis=1) * np.fft.fft(chirp[::-1], length)[None, :], axis=1
    )[:, : TAPS + CHIRP - 1]
    samples = SPAN * FRAME
    placed = np.zeros((2, samples, BANDS), np.complex128)
    for parity in range(2):
        first = (SPAN - 1) * FRAME + (parity + 1) * BANDS - (TAPS + CHIRP - 1)
        placed[parity, first : first + TAPS + CHIRP - 1] = filters.T
    real, imag = placed.real, placed.imag
    parts = np.stack(
        [np.stack([real, imag], axis=2), np.stack([-imag, real], axis=2)]
    )
    parts = parts.reshape(2, 2, SPAN, FRAME, 2, BANDS // 2, 2)
    parts = parts.transpose(2, 0, 3, 1, 6, 4, 5)
    return parts.reshape(SPAN, 2 * FRAME, 4 * BANDS).astype(np.float32).astype(ml_dtypes.bfloat16)


def kernel(
    count, x_ref, w_ref, o_ref, own, weight, tiles, total, times, turned, outgoing,
    own_sem, weight_sem, halo_send, halo_recv, send_sem, recv_sem, local_sem,
):
    me = lax.axis_index("tm")
    frames = own.shape[1] // FRAME - HALO
    half = frames // 2
    block = APART * 16

    load = pltpu.make_async_copy(
        x_ref, own.at[:, pl.ds(HALO * FRAME, frames * FRAME)], own_sem
    )
    load.start()

    def weight_load(group):
        piece = pl.ds(0, 1) if group is None else pl.ds(1 + group * GROUP, GROUP)
        sem = weight_sem.at[GROUPS if group is None else group]
        return pltpu.make_async_copy(w_ref.at[piece], weight.at[piece], sem)

    for group in reversed(range(GROUPS)):
        weight_load(group).start()
    weight_load(None).start()

    barrier = pltpu.get_barrier_semaphore()
    for shift in range(1, count):
        pl.semaphore_signal(
            barrier, inc=1, device_id={"tm": lax.rem(me + shift, count)}, device_id_type=MESH
        )

    def edge(group):
        first = 1 + group * GROUP if group else 0
        size = (HALO if group == GROUPS - 1 else 1 + (group + 1) * GROUP) - first
        return pltpu.make_async_remote_copy(
            src_ref=x_ref.at[:, pl.ds((frames - HALO + first) * FRAME, size * FRAME)],
            dst_ref=own.at[:, pl.ds(first * FRAME, size * FRAME)],
            send_sem=halo_send.at[group],
            recv_sem=halo_recv.at[group],
            device_id={"tm": lax.rem(me + 1, count)},
            device_id_type=MESH,
        )

    def greet():
        pl.semaphore_wait(barrier, count - 1)

        @pl.when(me < count - 1)
        def _():
            for group in reversed(range(GROUPS)):
                edge(group).start()

    def arrange(first, last):
        def one(index, carry):
            four = [
                own[:, pl.ds(pl.multiple_of((index + j * APART) * FRAME, FRAME), FRAME)].astype(
                    jnp.float32
                )
                for j in range(4)
            ]
            for rows in range(2):
                tiles[rows, index] = jnp.concatenate(
                    [
                        jnp.concatenate(
                            [f[part * 8 + rows * 4 : part * 8 + rows * 4 + 4] for f in four], axis=0
                        )
                        for part in range(2)
                    ],
                    axis=1,
                ).astype(jnp.bfloat16)
            return carry

        lax.fori_loop(first, last, one, 0, unroll=7)

    def product(side, rows, lag, amount):
        left = jnp.concatenate(
            [
                tiles[rows, pl.ds(side * half + lag + j, APART)].reshape(block, 2 * FRAME)
                for j in range(amount)
            ],
            axis=1,
        )
        right = weight[pl.ds(lag, amount)].reshape(amount * 2 * FRAME, 4 * BANDS)
        return jnp.dot(left, right, preferred_element_type=jnp.float32)

    def send(side, rows, chunk, shift):
        to = lax.rem(me + shift, count)
        start = pl.multiple_of((me * 2 + side) * frames, frames)
        return pltpu.make_async_remote_copy(
            src_ref=outgoing.at[chunk, :, to],
            dst_ref=o_ref.at[:, pl.ds(rows * 4, 4), :, pl.ds(start, frames)],
            send_sem=send_sem.at[chunk],
            recv_sem=recv_sem.at[chunk],
            device_id={"tm": to},
            device_id_type=MESH,
        )

    def keep(side, rows, chunk):
        start = pl.multiple_of((me * 2 + side) * frames, frames)
        return pltpu.make_async_copy(
            outgoing.at[chunk, :, me],
            o_ref.at[:, pl.ds(rows * 4, 4), :, pl.ds(start, frames)],
            local_sem.at[chunk],
        )

    load.wait()
    arrange(half, HALO + frames - 3 * APART)
    greet()

    def one_chunk(chunk, carry):
        side, rows = 1 - chunk // 2, chunk % 2
        total[...] = jnp.zeros_like(total)

        def one_group(step, carry):
            group = GROUPS - 1 - step

            @pl.when(chunk == 0)
            def _():
                weight_load(group).wait()

            for part in range(GROUPS):
                @pl.when((chunk == 2) & (group == part))
                def _():
                    @pl.when(me > 0)
                    def _():
                        edge(part).wait_recv()

                    if part == GROUPS - 1:
                        @pl.when(me == 0)
                        def _():
                            own[:, : HALO * FRAME] = jnp.zeros((16, HALO * FRAME), own.dtype)

                    arrange(
                        1 + part * GROUP if part else 0,
                        HALO + APART if part == GROUPS - 1 else 1 + (part + 1) * GROUP,
                    )

            total[...] += product(side, rows, 1 + group * GROUP, GROUP)
            return carry

        lax.fori_loop(0, GROUPS, one_group, 0)

        @pl.when(chunk == 0)
        def _():
            weight_load(None).wait()

        total[...] += product(side, rows, 0, 1)

        for v in range(APART):
            for upper in range(2):
                for parity in range(2):
                    row = (upper * 2 * APART + v * 2 + parity) * 8
                    times[row : row + 8, :] = total[
                        v * 16 + upper * 8 : v * 16 + upper * 8 + 8,
                        parity * 128 : parity * 128 + 128,
                    ]
        for r in range(4):
            across = jnp.concatenate(
                [
                    times[pl.ds(j // 2 * 16 * APART + j % 2 * 4 + r, 2 * APART, stride=8), :]
                    for j in range(4)
                ],
                axis=0,
            ).T
            for band in range(2):
                turned[pl.ds(2 * r + band, 2 * count, stride=8), :] = across[
                    band * 64 : band * 64 + 64
                ]
        outgoing[chunk] = turned[...].astype(jnp.bfloat16).reshape(2, count, 4, 2, frames)
        for shift in sorted(range(1, count), key=lambda s: (s % 8 < 4, -min(s % 8, 8 - s % 8))):
            send(side, rows, chunk, shift).start()
        keep(side, rows, chunk).start()
        return carry

    lax.fori_loop(0, 4, one_chunk, 0)

    @pl.when(me < count - 1)
    def _():
        for group in range(GROUPS):
            edge(group).wait_send()

    def finish(chunk, carry):
        side, rows = 1 - chunk // 2, chunk % 2
        others = outgoing.at[chunk, :, pl.ds(0, count - 1)]
        pltpu.make_async_copy(others, others, recv_sem.at[chunk]).wait()
        pltpu.make_async_copy(others, others, send_sem.at[chunk]).wait()
        keep(side, rows, chunk).wait()
        return carry

    lax.fori_loop(0, 4, finish, 0)


def solution(mesh):
    count = mesh.shape["tm"]
    table = weights()

    def shards(echoes):
        parts, rows, samples = echoes.shape
        frames = samples // FRAME
        result = pl.pallas_call(
            lambda *refs: kernel(count, *refs),
            out_shape=pltpu.VMEM((2, rows, 2, count * 2 * frames), jnp.bfloat16),
            in_specs=[pl.BlockSpec(memory_space=pl.ANY)] * 2,
            out_specs=pl.BlockSpec(memory_space=pltpu.VMEM),
            scratch_shapes=[
                pltpu.VMEM((16, HALO * FRAME + samples), jnp.bfloat16),
                pltpu.VMEM(table.shape, jnp.bfloat16),
                pltpu.VMEM((2, HALO + frames - 3 * APART, 16, 2 * FRAME), jnp.bfloat16),
                pltpu.VMEM((APART * 16, 4 * BANDS), jnp.float32),
                pltpu.VMEM((frames * 4, 2 * BANDS), jnp.float32),
                pltpu.VMEM((2 * count * 8, frames), jnp.float32),
                pltpu.VMEM((4, 2, count, 4, 2, frames), jnp.bfloat16),
                pltpu.SemaphoreType.DMA,
                pltpu.SemaphoreType.DMA((GROUPS + 1,)),
                pltpu.SemaphoreType.DMA((GROUPS,)),
                pltpu.SemaphoreType.DMA((GROUPS,)),
                pltpu.SemaphoreType.DMA((4,)),
                pltpu.SemaphoreType.DMA((4,)),
                pltpu.SemaphoreType.DMA((4,)),
            ],
            compiler_params=pltpu.CompilerParams(
                collective_id=0, has_side_effects=True, vmem_limit_bytes=60 << 20
            ),
            name="radar",
        )(echoes.reshape(parts * rows, samples), jnp.asarray(table))
        return result

    return jax.shard_map(
        shards,
        mesh=mesh,
        in_specs=(P(None, "cp", "tm"),),
        out_specs=P(None, "cp", "tm", None),
        check_vma=False,
    )
```

```python
import math

import jax
import jax.numpy as jnp
import ml_dtypes
import numpy as np
from jax import lax
from jax.experimental import pallas as pl
from jax.experimental.pallas import tpu as pltpu
from jax.sharding import PartitionSpec as P

CHIRP = 1024
BANDS = 64
TAPS = 4096
MESH = pl.DeviceIdType.MESH

FRAME = 128
SPAN = 41
HALO = SPAN - 1
GROUP = 20
GROUPS = (SPAN - 1) // GROUP
APART = 16


def rounded(values):
    return np.asarray(values, np.float64).astype(ml_dtypes.bfloat16).astype(np.float64)


def weights():
    lag = np.arange(CHIRP)
    phase = math.pi * ((lag - CHIRP // 2) ** 2 % (2 * CHIRP)) / CHIRP
    scale = 1.0 / math.sqrt(CHIRP)
    chirp = rounded(np.cos(phase) * scale) + 1j * rounded(np.sin(phase) * scale)
    tap = np.arange(TAPS)
    window = 0.5 - 0.5 * np.cos(2.0 * np.pi * (tap + 0.5) / TAPS)
    prototype = rounded(np.sinc((tap - (TAPS - 1) / 2.0) / BANDS) * window / math.sqrt(BANDS))
    column = np.arange(BANDS)
    angle = 2.0 * np.pi * (column[:, None] * column[None, :] % BANDS) / BANDS
    table = rounded(np.cos(angle)) - 1j * rounded(np.sin(angle))
    modulated = prototype[None, :] * np.tile(table, (1, TAPS // BANDS))
    length = 2 * TAPS
    filters = np.fft.ifft(
        np.fft.fft(modulated, length, axis=1) * np.fft.fft(chirp[::-1], length)[None, :], axis=1
    )[:, : TAPS + CHIRP - 1]
    samples = SPAN * FRAME
    placed = np.zeros((2, samples, BANDS), np.complex128)
    for parity in range(2):
        first = (SPAN - 1) * FRAME + (parity + 1) * BANDS - (TAPS + CHIRP - 1)
        placed[parity, first : first + TAPS + CHIRP - 1] = filters.T
    real, imag = placed.real, placed.imag
    parts = np.stack(
        [np.stack([real, imag], axis=2), np.stack([-imag, real], axis=2)]
    )
    parts = parts.reshape(2, 2, SPAN, FRAME, 2, BANDS // 2, 2)
    parts = parts.transpose(2, 0, 3, 1, 6, 4, 5)
    return parts.reshape(SPAN, 2 * FRAME, 4 * BANDS).astype(np.float32).astype(ml_dtypes.bfloat16)


def kernel(
    count, x_ref, w_ref, o_ref, own, weight, tiles, total, times, turned, outgoing,
    own_sem, weight_sem, halo_send, halo_recv, send_sem, recv_sem, local_sem,
):
    me = lax.axis_index("tm")
    frames = own.shape[1] // FRAME - HALO
    half = frames // 2
    block = APART * 16

    load = pltpu.make_async_copy(
        x_ref, own.at[:, pl.ds(HALO * FRAME, frames * FRAME)], own_sem
    )
    load.start()

    def weight_load(group):
        piece = pl.ds(0, 1) if group is None else pl.ds(1 + group * GROUP, GROUP)
        sem = weight_sem.at[GROUPS if group is None else group]
        return pltpu.make_async_copy(w_ref.at[piece], weight.at[piece], sem)

    for group in reversed(range(GROUPS)):
        weight_load(group).start()
    weight_load(None).start()

    barrier = pltpu.get_barrier_semaphore()
    for shift in range(1, count):
        pl.semaphore_signal(
            barrier, inc=1, device_id={"tm": lax.rem(me + shift, count)}, device_id_type=MESH
        )

    def edge(group):
        first = 1 + group * GROUP if group else 0
        size = (HALO if group == GROUPS - 1 else 1 + (group + 1) * GROUP) - first
        return pltpu.make_async_remote_copy(
            src_ref=x_ref.at[:, pl.ds((frames - HALO + first) * FRAME, size * FRAME)],
            dst_ref=own.at[:, pl.ds(first * FRAME, size * FRAME)],
            send_sem=halo_send.at[group],
            recv_sem=halo_recv.at[group],
            device_id={"tm": lax.rem(me + 1, count)},
            device_id_type=MESH,
        )

    def greet():
        pl.semaphore_wait(barrier, count - 1)

        @pl.when(me < count - 1)
        def _():
            for group in reversed(range(GROUPS)):
                edge(group).start()

    def arrange(first, last):
        def one(index, carry):
            four = [
                own[:, pl.ds(pl.multiple_of((index + j * APART) * FRAME, FRAME), FRAME)].astype(
                    jnp.float32
                )
                for j in range(4)
            ]
            for rows in range(2):
                tiles[rows, index] = jnp.concatenate(
                    [
                        jnp.concatenate(
                            [f[part * 8 + rows * 4 : part * 8 + rows * 4 + 4] for f in four], axis=0
                        )
                        for part in range(2)
                    ],
                    axis=1,
                ).astype(jnp.bfloat16)
            return carry

        lax.fori_loop(first, last, one, 0, unroll=7)

    def product(side, rows, lag, amount):
        left = jnp.concatenate(
            [
                tiles[rows, pl.ds(side * half + lag + j, APART)].reshape(block, 2 * FRAME)
                for j in range(amount)
            ],
            axis=1,
        )
        right = weight[pl.ds(lag, amount)].reshape(amount * 2 * FRAME, 4 * BANDS)
        return jnp.dot(left, right, preferred_element_type=jnp.float32)

    def send(side, rows, chunk, shift):
        to = lax.rem(me + shift, count)
        start = pl.multiple_of((me * 2 + side) * frames, frames)
        return pltpu.make_async_remote_copy(
            src_ref=outgoing.at[chunk, :, to],
            dst_ref=o_ref.at[:, pl.ds(rows * 4, 4), :, pl.ds(start, frames)],
            send_sem=send_sem.at[chunk],
            recv_sem=recv_sem.at[chunk],
            device_id={"tm": to},
            device_id_type=MESH,
        )

    def keep(side, rows, chunk):
        start = pl.multiple_of((me * 2 + side) * frames, frames)
        return pltpu.make_async_copy(
            outgoing.at[chunk, :, me],
            o_ref.at[:, pl.ds(rows * 4, 4), :, pl.ds(start, frames)],
            local_sem.at[chunk],
        )

    greet()
    load.wait()
    arrange(half, HALO + frames - 3 * APART)

    def one_chunk(chunk, carry):
        side, rows = 1 - chunk // 2, chunk % 2
        total[...] = jnp.zeros_like(total)

        def one_group(step, carry):
            group = GROUPS - 1 - step

            @pl.when(chunk == 0)
            def _():
                weight_load(group).wait()

            for part in range(GROUPS):
                @pl.when((chunk == 2) & (group == part))
                def _():
                    @pl.when(me > 0)
                    def _():
                        edge(part).wait_recv()

                    if part == GROUPS - 1:
                        @pl.when(me == 0)
                        def _():
                            own[:, : HALO * FRAME] = jnp.zeros((16, HALO * FRAME), own.dtype)

                    arrange(
                        1 + part * GROUP if part else 0,
                        HALO + APART if part == GROUPS - 1 else 1 + (part + 1) * GROUP,
                    )

            total[...] += product(side, rows, 1 + group * GROUP, GROUP)
            return carry

        lax.fori_loop(0, GROUPS, one_group, 0)

        @pl.when(chunk == 0)
        def _():
            weight_load(None).wait()

        total[...] += product(side, rows, 0, 1)

        for v in range(APART):
            for upper in range(2):
                for parity in range(2):
                    row = (upper * 2 * APART + v * 2 + parity) * 8
                    times[row : row + 8, :] = total[
                        v * 16 + upper * 8 : v * 16 + upper * 8 + 8,
                        parity * 128 : parity * 128 + 128,
                    ]
        for r in range(4):
            across = jnp.concatenate(
                [
                    times[pl.ds(j // 2 * 16 * APART + j % 2 * 4 + r, 2 * APART, stride=8), :]
                    for j in range(4)
                ],
                axis=0,
            ).T
            for band in range(2):
                turned[pl.ds(2 * r + band, 2 * count, stride=8), :] = across[
                    band * 64 : band * 64 + 64
                ]
        outgoing[chunk] = turned[...].astype(jnp.bfloat16).reshape(2, count, 4, 2, frames)
        for shift in sorted(range(1, count), key=lambda s: (s % 8 < 4, -min(s % 8, 8 - s % 8))):
            send(side, rows, chunk, shift).start()
        keep(side, rows, chunk).start()
        return carry

    lax.fori_loop(0, 4, one_chunk, 0)

    @pl.when(me < count - 1)
    def _():
        for group in range(GROUPS):
            edge(group).wait_send()

    def finish(chunk, carry):
        side, rows = 1 - chunk // 2, chunk % 2
        others = outgoing.at[chunk, :, pl.ds(0, count - 1)]
        pltpu.make_async_copy(others, others, recv_sem.at[chunk]).wait()
        pltpu.make_async_copy(others, others, send_sem.at[chunk]).wait()
        keep(side, rows, chunk).wait()
        return carry

    lax.fori_loop(0, 4, finish, 0)


def solution(mesh):
    count = mesh.shape["tm"]
    table = weights()

    def shards(echoes):
        parts, rows, samples = echoes.shape
        frames = samples // FRAME
        result = pl.pallas_call(
            lambda *refs: kernel(count, *refs),
            out_shape=pltpu.VMEM((2, rows, 2, count * 2 * frames), jnp.bfloat16),
            in_specs=[pl.BlockSpec(memory_space=pl.ANY)] * 2,
            out_specs=pl.BlockSpec(memory_space=pltpu.VMEM),
            scratch_shapes=[
                pltpu.VMEM((16, HALO * FRAME + samples), jnp.bfloat16),
                pltpu.VMEM(table.shape, jnp.bfloat16),
                pltpu.VMEM((2, HALO + frames - 3 * APART, 16, 2 * FRAME), jnp.bfloat16),
                pltpu.VMEM((APART * 16, 4 * BANDS), jnp.float32),
                pltpu.VMEM((frames * 4, 2 * BANDS), jnp.float32),
                pltpu.VMEM((2 * count * 8, frames), jnp.float32),
                pltpu.VMEM((4, 2, count, 4, 2, frames), jnp.bfloat16),
                pltpu.SemaphoreType.DMA,
                pltpu.SemaphoreType.DMA((GROUPS + 1,)),
                pltpu.SemaphoreType.DMA((GROUPS,)),
                pltpu.SemaphoreType.DMA((GROUPS,)),
                pltpu.SemaphoreType.DMA((4,)),
                pltpu.SemaphoreType.DMA((4,)),
                pltpu.SemaphoreType.DMA((4,)),
            ],
            compiler_params=pltpu.CompilerParams(
                collective_id=0, has_side_effects=True, vmem_limit_bytes=60 << 20
            ),
            name="radar",
        )(echoes.reshape(parts * rows, samples), jnp.asarray(table))
        return result

    return jax.shard_map(
        shards,
        mesh=mesh,
        in_specs=(P(None, "cp", "tm"),),
        out_specs=P(None, "cp", "tm", None),
        check_vma=False,
    )
```
